32 devices in a mesh: groups: 1, expert: 16 (over z, y, x), sub: 2 (over core).
Axes of the slice: x: 2, y: 2, z: 4, core: 2. Of those that a mesh axis runs over, the one named last changes fastest.
Arguments:
- tokens: bfloat16 [1024, 3584], P(('groups', 'expert', 'sub')), may hold values from -6 to 6
- gate_weight: bfloat16 [16, 3584, 1024], P('expert', None, 'sub'), may hold values from -0.09375 to 0.09375
- up_weight: bfloat16 [16, 3584, 1024], P('expert', None, 'sub'), may hold values from -0.09375 to 0.09375
- down_weight: bfloat16 [16, 1024, 3584], P('expert', 'sub'), may hold values from -0.1875 to 0.1875
- expert_ids: int32 [1024, 8], P(('groups', 'expert', 'sub')), may hold values from 0 to 15, all different within a row; in each aligned block of 32 rows (0 to 31, 32 to 63, ...) at most 32 rows name the same one
- gate_fixed: int32 [1024, 8], P(('groups', 'expert', 'sub')), may hold values from 1 to 65535
Outputs:
- mixed_out: bfloat16 [1024, 3584], P(('groups', 'expert', 'sub'))
The draws below stay inside these ranges and needn't reach their ends.
Inputs may be any that keep to these rules, and one draw needn't show every extreme that they name: `expert_ids`: each row names 8 different experts; among the 32 rows of one device no expert is named more than 32 times, a bound that some block reaches.
All inputs are finite; a program needn't handle non-finite values.
Results may differ from the reference program's by a relative error of at most 0.0058.
Values may be sent and summed in bfloat16 or wider, within the bound.
No kernel may reach another device: no remote copies, remote signals or barrier semaphores. Data moves between devices by JAX's collectives and lax.ppermute only.
A program may use at most 128 MiB of HBM per device.

```python
import math
import jax
import jax.numpy as jnp
import numpy as np
from jax import lax

D = 3584
FF_E = 1024
TOPK = 8
TOK_DEV = 32
EXPERTS = 16
CAP = 32
TOKENS = 1024
N_EXPERT = 16
N_SUB = 2


def touch_ends(drawn, own_key, low, largest):
    index_at = [jax.random.randint(jax.random.fold_in(own_key, axis), (), 0, length) for axis, length in enumerate(drawn.shape)]
    longest = drawn.shape.index(max(drawn.shape))
    next_to = index_at[:longest] + [(index_at[longest] + 1) % drawn.shape[longest]] + index_at[longest + 1:]
    return drawn.at[tuple(index_at)].set(low).at[tuple(next_to)].set(largest)


def shard_levels(own_key, shape, pieces, low, high):
    def one(position, blocks):
        draws = jax.random.uniform(jax.random.fold_in(jax.random.fold_in(own_key, 6), position), (blocks,), jnp.float32, low / len(pieces), high / len(pieces))
        return jnp.repeat(jnp.exp(draws), shape[position] // blocks).reshape((-1,) + (1,) * (len(shape) - position - 1))

    level = one(*pieces[0])
    for cut in pieces[1:]:
        level = level * one(*cut)
    return level


def assign_block(stream_key, own, number, rows, count, top, limit, skew):
    order = jax.random.permutation(stream_key, count)
    heavy_load, common = shares(count, rows * top, limit, skew, True), shares(count, rows * top, limit, skew, False)
    places = jnp.arange(count)

    def named(lengths, rotation):
        used = int((lengths > 0).sum())
        fixed = max(1, used // 4)
        shifted = fixed + (places - fixed + rotation * (used - fixed)) % max(1, count - fixed)
        return jnp.zeros((count,), jnp.int32).at[order[jnp.where(places < fixed, places, shifted)]].set(jnp.asarray(lengths, jnp.int32))

    lengths = jnp.where(number % 4 == 0, named(heavy_load, number // 4), named(common, number - number // 4 - 1))
    mixed = jax.random.permutation(jax.random.fold_in(own, 3), count)
    source_of, taker = mixed[0:count // 2 * 2:2], mixed[1:count // 2 * 2:2]
    slack = jnp.minimum(lengths[source_of] - 1, limit - lengths[taker]) // 2
    slack = jnp.where((source_of == order[0]) | (taker == order[0]) | (lengths[taker] == 0), 0, jnp.maximum(slack, 0))
    shifted = jax.random.randint(jax.random.fold_in(own, 4), (count // 2,), 0, 1 << 20) % (slack + 1)
    lengths = lengths.at[source_of].add(-shifted).at[taker].add(shifted)
    members = jnp.searchsorted(jnp.cumsum(lengths), jnp.arange(rows * top), side="right").astype(jnp.int32)
    listing = members.reshape(top, rows).T
    listing = listing[jax.random.permutation(jax.random.fold_in(own, 1), rows)]
    rotation = jax.random.randint(jax.random.fold_in(own, 2), (rows, 1), 0, top)
    return jnp.take_along_axis(listing, (jnp.arange(top)[None, :] + rotation) % top, axis=1)


def shares(count, total, most, lean, full):
    weights = [(1 << 20) // math.isqrt(rank ** lean) + 1 for rank in range(1, count + 1)]
    largest = most if full else min(most, max(-(-total // count), total * weights[0] // sum(weights)))
    least = 1 if total - largest >= count - 1 else 0
    counts, surplus = [largest] + [least] * (count - 1), total - largest - least * (count - 1)
    while surplus > 0:
        movable = [i for i in range(1, count) if counts[i] < largest] or [i for i in range(1, count) if counts[i] < most]
        mass, budget = sum([weights[i] for i in movable]), surplus
        for i in movable:
            extra = min(most - counts[i], max(1, budget * weights[i] // mass), surplus)
            counts[i] = counts[i] + extra
            surplus = surplus - extra
    return np.array(counts)


def bell_draw(own_key, extent, scale, most, shards=(), kind=jnp.bfloat16):
    entries = jax.random.normal(own_key, extent, jnp.float32) * scale
    if len(shards) > 0:
        entries = shard_levels(own_key, extent, shards, -0.22, 0.18) * entries
    return jnp.clip(entries, min=-most, max=most).astype(kind)


def setup_inputs(seed: int = 0, part: int = 0) -> dict:
    key_list = jax.random.split(jax.random.key(seed), 7)
    part_keys = jax.random.split(jax.random.fold_in(key_list[6], part), 7)
    tokens = bell_draw(part_keys[0], (TOKENS, D), 1.0, 6.0, ((0, 32),))
    gate_weight = bell_draw(key_list[1], (EXPERTS, D, FF_E), D ** -0.5, 0.09375, ((0, 16), (2, 2)))
    up_weight = bell_draw(key_list[2], (EXPERTS, D, FF_E), D ** -0.5, 0.09375, ((0, 16), (2, 2)))
    down_weight = bell_draw(key_list[3], (EXPERTS, FF_E, D), FF_E ** -0.5, 0.1875, ((0, 16), (1, 2)))
    expert_ids_keys = jax.random.split(jax.random.fold_in(part_keys[4], 1), TOKENS // TOK_DEV)
    expert_ids_turns = jax.random.permutation(jax.random.fold_in(part_keys[4], 3), TOKENS // TOK_DEV)
    expert_ids = jax.vmap(lambda own, number: assign_block(jax.random.fold_in(part_keys[4], 2), own, number, TOK_DEV, EXPERTS, TOPK, CAP, 1))(expert_ids_keys, expert_ids_turns).reshape((TOKENS, TOPK))
    gate_fixed = touch_ends(jax.random.randint(part_keys[5], (TOKENS, TOPK), 1, 65536), jax.random.fold_in(part_keys[5], 1), 1, 65535).astype(jnp.int32)
    return dict(tokens=tokens, gate_weight=gate_weight, up_weight=up_weight, down_weight=down_weight, expert_ids=expert_ids, gate_fixed=gate_fixed)


def reference(tokens, gate_weight, up_weight, down_weight, expert_ids, gate_fixed):
    devices = N_EXPERT * N_SUB
    routes = expert_ids.reshape(devices, TOK_DEV * TOPK)
    onehot = (routes[:, :, None] == jnp.arange(EXPERTS, dtype=jnp.int32)[None, None, :]).astype(jnp.int32)
    ordinal = (jnp.sum(jnp.cumsum(onehot, axis=1) * onehot, axis=2) - 1).astype(jnp.int32)
    source = (jnp.arange(devices, dtype=jnp.int32)[:, None] * jnp.ones_like(routes)).astype(jnp.int32)
    token_index = (source * TOK_DEV + jnp.arange(TOK_DEV * TOPK, dtype=jnp.int32)[None, :] // TOPK).astype(jnp.int32)
    table = jnp.zeros((EXPERTS, devices, CAP), jnp.int32).at[routes, source, ordinal].set(token_index)

    def per_expert(operands):
        index_block, w_gate, w_up, w_down = operands
        row_block = jnp.take(tokens, index_block.reshape(-1), axis=0)
        gate_proj = jnp.dot(row_block, w_gate, preferred_element_type=jnp.float32)
        up_proj = jnp.dot(row_block, w_up, preferred_element_type=jnp.float32)
        hidden = (jax.nn.silu(gate_proj) * up_proj).astype(jnp.bfloat16)
        result = jnp.dot(hidden, w_down, preferred_element_type=jnp.float32).astype(jnp.bfloat16)
        return result.reshape(devices, CAP, D)

    outputs = lax.map(per_expert, (table, gate_weight, up_weight, down_weight))
    picked = outputs[routes, source, ordinal].reshape(TOKENS, TOPK, D).astype(jnp.float32)
    fixed_point = gate_fixed.astype(jnp.float32)
    route_weight = fixed_point / jnp.sum(fixed_point, axis=1, keepdims=True)
    mixed_out = jnp.sum(picked * route_weight[:, :, None], axis=1)
    return mixed_out.astype(jnp.bfloat16)
```

```python
import jax
import jax.numpy as jnp
from jax import lax
from jax.sharding import PartitionSpec as P

LANES = 128
DEPTH_TILE = 256


def plan(experts, feature_count):
    bits = experts.bit_length() - 1
    if experts == 16:
        orders = ((3, 2, 0, 1), (0, 3, 2, 1), (3, 2, 1, 0), (1, 3, 2, 0))
        mirror = (1, 0, 2, 3)
    else:
        orders = tuple(tuple((turn + step) % bits for step in range(bits)) for turn in range(0, bits, max(1, bits // 4)))[:4]
        half = bits // 2
        mirror = tuple((bit + half) % bits if bits % 2 == 0 else bit for bit in range(bits))
    tiles = feature_count // DEPTH_TILE
    count = len(orders)
    widths = [DEPTH_TILE * (tiles // count + (1 if i < tiles % count else 0)) for i in range(count)]
    widths[-1] += feature_count - sum(widths)
    return orders, mirror, widths


def cross(block, bit, experts, mirror):
    pairs = []
    for chip in range(experts):
        for core, flipped in ((0, bit), (1, mirror[bit])):
            pairs.append((chip * 2 + core, (chip ^ (1 << flipped)) * 2 + core))
    return lax.ppermute(block, ("expert", "sub"), pairs)


def other_core(block):
    return lax.ppermute(block, "sub", [(0, 1), (1, 0)])


def per_device(tokens, gate_weight, up_weight, down_weight, expert_ids, gate_fixed):
    experts = lax.axis_size("expert")
    bits = experts.bit_length() - 1
    tok_rows, top_count = expert_ids.shape
    feature_count = tokens.shape[1]
    orders, mirror, widths = plan(experts, feature_count)
    starts = [sum(widths[:i]) for i in range(len(widths))]
    rows = experts * tok_rows

    fixed_point = gate_fixed.astype(jnp.float32)
    route_share = fixed_point / jnp.sum(fixed_point, axis=1, keepdims=True)
    chosen = expert_ids[:, :, None] == jnp.arange(experts, dtype=jnp.int32)[None, None, :]
    dense_share = jnp.sum(jnp.where(chosen, route_share[:, :, None], 0.0), axis=1)
    high = lax.reduce_precision(dense_share, 8, 7)
    low = dense_share - high
    shares = jnp.concatenate([high, low], axis=1)
    shares = jnp.pad(shares, ((0, 0), (0, -2 * experts % LANES))).astype(jnp.bfloat16)

    own = [w[0] for w in (gate_weight, up_weight, down_weight)]
    far = [other_core(w) for w in own]

    held = []
    for start, width in zip(starts, widths):
        piece = tokens[:, start : start + width]
        if start == 0:
            piece = jnp.concatenate([piece, shares], axis=1)
        held.append(piece.reshape((1,) * bits + piece.shape))
    for step in range(bits):
        for i, order in enumerate(orders):
            held[i] = jnp.concatenate([held[i], cross(held[i], order[step], experts, mirror)], axis=order[step])
    held = [piece.reshape(rows, -1) for piece in held]

    mine = lax.axis_index("expert")
    lane = jnp.arange(shares.shape[1], dtype=jnp.int32)
    picked = (lane == mine) | (lane == mine + experts)
    weight = jnp.sum(jnp.where(picked[None, :], held[0][:, widths[0] :].astype(jnp.float32), 0.0), axis=1, keepdims=True)
    held[0] = held[0][:, : widths[0]]
    x = jnp.concatenate(held, axis=1)

    hidden = []
    for w in (own, far):
        gate_proj = jnp.dot(x, w[0], preferred_element_type=jnp.float32)
        up_proj = jnp.dot(x, w[1], preferred_element_type=jnp.float32)
        hidden.append((jax.nn.silu(gate_proj) * up_proj).astype(jnp.bfloat16))

    sums = []
    for start, width in zip(starts, widths):
        part = sum(jnp.dot(h, w[2][:, start : start + width], preferred_element_type=jnp.float32) for h, w in zip(hidden, (own, far)))
        sums.append((part * weight).astype(jnp.bfloat16).reshape((2,) * bits + (tok_rows, width)))
    for step in reversed(range(bits)):
        for i, order in enumerate(orders):
            axis = order[step]
            keep = lax.slice_in_dim(sums[i], 0, 1, axis=axis)
            arrived = cross(lax.slice_in_dim(sums[i], 1, 2, axis=axis), axis, experts, mirror)
            sums[i] = (keep.astype(jnp.float32) + arrived.astype(jnp.float32)).astype(jnp.bfloat16)
    return jnp.concatenate([part.reshape(tok_rows, -1) for part in sums], axis=1)


def solution(mesh):
    in_specs = (
        P(("groups", "expert", "sub"), None),
        P("expert", None, "sub"),
        P("expert", None, "sub"),
        P("expert", "sub", None),
        P(("groups", "expert", "sub"), None),
        P(("groups", "expert", "sub"), None),
    )
    out_specs = P(("groups", "expert", "sub"), None)
    return jax.shard_map(
        per_device, mesh=mesh, in_specs=in_specs, out_specs=out_specs, check_vma=False
    )
```

```python
import jax
import jax.numpy as jnp
from jax import lax
from jax.sharding import PartitionSpec as P

LANES = 128
DEPTH_TILE = 256


def split(feature_count, parts):
    tiles = feature_count // DEPTH_TILE
    edges = [DEPTH_TILE * (tiles * sum(parts[:i]) // sum(parts)) for i in range(len(parts))] + [feature_count]
    return [(low, high - low) for low, high in zip(edges, edges[1:])]


def plan(experts):
    bits = experts.bit_length() - 1
    if experts == 16:
        gather = (((3, 0, 1, 2), 5), ((3, 1, 2, 0), 5), ((3, 2, 0, 1), 4))
        reduce = (((3, 0, 2, 1), 4), ((2, 3, 0, 1), 5), ((3, 0, 1, 2), 5))
        mirror = (1, 0, 2, 3)
    else:
        turns = range(0, bits, max(1, bits // 4))
        gather = tuple((tuple((turn + step) % bits for step in range(bits)), 1) for turn in turns)[:4]
        reduce = gather
        half = bits // 2
        mirror = tuple((bit + half) % bits if bits % 2 == 0 else bit for bit in range(bits))
    return gather, reduce, mirror


def cross(block, bit, experts, mirror):
    pairs = []
    for chip in range(experts):
        for core, flipped in ((0, bit), (1, mirror[bit])):
            pairs.append((chip * 2 + core, (chip ^ (1 << flipped)) * 2 + core))
    return lax.ppermute(block, ("expert", "sub"), pairs)


def other_core(block):
    return lax.ppermute(block, "sub", [(0, 1), (1, 0)])


def per_device(tokens, gate_weight, up_weight, down_weight, expert_ids, gate_fixed):
    experts = lax.axis_size("expert")
    bits = experts.bit_length() - 1
    tok_rows, top_count = expert_ids.shape
    feature_count = tokens.shape[1]
    gather, reduce, mirror = plan(experts)
    columns = split(feature_count, [share for _, share in gather])
    rows = experts * tok_rows

    fixed_point = gate_fixed.astype(jnp.float32)
    route_share = fixed_point / jnp.sum(fixed_point, axis=1, keepdims=True)
    chosen = expert_ids[:, :, None] == jnp.arange(experts, dtype=jnp.int32)[None, None, :]
    dense_share = jnp.sum(jnp.where(chosen, route_share[:, :, None], 0.0), axis=1)
    high = lax.reduce_precision(dense_share, 8, 7)
    low = dense_share - high
    shares = jnp.concatenate([high, low], axis=1)
    shares = jnp.pad(shares, ((0, 0), (0, -2 * experts % LANES))).astype(jnp.bfloat16)

    own = [w[0] for w in (gate_weight, up_weight, down_weight)]
    far = [other_core(w) for w in own]

    held = []
    for start, width in columns:
        piece = tokens[:, start : start + width]
        if start + width == feature_count:
            piece = jnp.concatenate([piece, shares], axis=1)
        held.append(piece.reshape((1,) * bits + piece.shape))
    for step in range(bits):
        for i, (order, _) in enumerate(gather):
            axis = order[step]
            held[i] = jnp.concatenate([held[i], cross(held[i], axis, experts, mirror)], axis=axis)
    held = [piece.reshape(rows, -1) for piece in held]

    mine = lax.axis_index("expert")
    lane = jnp.arange(shares.shape[1], dtype=jnp.int32)
    picked = (lane == mine) | (lane == mine + experts)
    weight = jnp.sum(jnp.where(picked[None, :], held[-1][:, columns[-1][1] :].astype(jnp.float32), 0.0), axis=1, keepdims=True)

    def project(matrix):
        total = None
        for i in (len(columns) - 1,) + tuple(range(len(columns) - 1)):
            start, width = columns[i]
            part = jnp.dot(held[i][:, :width], matrix[start : start + width], preferred_element_type=jnp.float32)
            total = part if total is None else total + part
        return total

    hidden = [(jax.nn.silu(project(w[0])) * project(w[1])).astype(jnp.bfloat16) for w in (own, far)]

    sums = []
    for start, width in split(feature_count, [share for _, share in reduce]):
        part = sum(
            jnp.dot(h, w[2][:, start : start + width], preferred_element_type=jnp.float32)
            for h, w in zip(hidden, (own, far))
        )
        sums.append((part * weight).astype(jnp.bfloat16).reshape((2,) * bits + (tok_rows, width)))
    sums = lax.optimization_barrier(sums)
    for step in reversed(range(bits)):
        for i, (order, _) in enumerate(reduce):
            axis = order[step]
            keep = lax.slice_in_dim(sums[i], 0, 1, axis=axis)
            arrived = cross(lax.slice_in_dim(sums[i], 1, 2, axis=axis), axis, experts, mirror)
            sums[i] = (keep.astype(jnp.float32) + arrived.astype(jnp.float32)).astype(jnp.bfloat16)
    return jnp.concatenate([part.reshape(tok_rows, -1) for part in sums], axis=1)


def solution(mesh):
    in_specs = (
        P(("groups", "expert", "sub"), None),
        P("expert", None, "sub"),
        P("expert", None, "sub"),
        P("expert", "sub", None),
        P(("groups", "expert", "sub"), None),
        P(("groups", "expert", "sub"), None),
    )
    out_specs = P(("groups", "expert", "sub"), None)
    return jax.shard_map(
        per_device, mesh=mesh, in_specs=in_specs, out_specs=out_specs, check_vma=False
    )
```

```python
import functools

import jax
import jax.numpy as jnp
from jax import lax
from jax.experimental import pallas as pl
from jax.sharding import PartitionSpec as P

LANES = 128
DEPTH_TILE = 256


def split(feature_count, parts):
    tiles = feature_count // DEPTH_TILE
    edges = [DEPTH_TILE * (tiles * sum(parts[:i]) // sum(parts)) for i in range(len(parts))] + [feature_count]
    return [(low, high - low) for low, high in zip(edges, edges[1:])]


def plan(experts):
    bits = experts.bit_length() - 1
    if experts == 16:
        gather = (((3, 0, 1, 2), 5), ((3, 1, 2, 0), 5), ((3, 2, 0, 1), 4))
        reduce = (((3, 0, 2, 1), 4), ((2, 3, 0, 1), 5), ((3, 0, 1, 2), 5))
        mirror = (1, 0, 2, 3)
    else:
        turns = range(0, bits, max(1, bits // 4))
        gather = tuple((tuple((turn + step) % bits for step in range(bits)), 1) for turn in turns)[:4]
        reduce = gather
        half = bits // 2
        mirror = tuple((bit + half) % bits if bits % 2 == 0 else bit for bit in range(bits))
    return gather, reduce, mirror


def cross(block, bit, experts, mirror):
    pairs = []
    for chip in range(experts):
        for core, flipped in ((0, bit), (1, mirror[bit])):
            pairs.append((chip * 2 + core, (chip ^ (1 << flipped)) * 2 + core))
    return lax.ppermute(block, ("expert", "sub"), pairs)


def other_core(block):
    return lax.ppermute(block, "sub", [(0, 1), (1, 0)])


def piece_kernel(columns, experts, tokens_ref, ids_ref, fixed_ref, *out_refs):
    for out_ref, (start, width) in zip(out_refs, columns):
        out_ref[:, :width] = tokens_ref[:, start : start + width]
    last_ref, width = out_refs[-1], columns[-1][1]
    fixed_point = fixed_ref[...].T.astype(jnp.float32)
    ids = ids_ref[...].T
    share = fixed_point / jnp.sum(fixed_point, axis=1, keepdims=True)
    lane = lax.broadcasted_iota(jnp.int32, (tokens_ref.shape[0], last_ref.shape[1] - width), 1)
    expert = jnp.where(lane < experts, lane, lane - experts)
    dense = jnp.zeros(lane.shape, jnp.float32)
    for k in range(share.shape[1]):
        dense = dense + jnp.where(expert == ids[:, k : k + 1], share[:, k : k + 1], 0.0)
    high = dense.astype(jnp.bfloat16).astype(jnp.float32)
    last_ref[:, width:] = jnp.where(lane < experts, high, dense - high).astype(last_ref.dtype)


def cut_pieces(tokens, expert_ids, gate_fixed, columns, experts):
    tok_rows = tokens.shape[0]
    extra = -(-2 * experts // LANES) * LANES
    widths = [width for _, width in columns]
    widths[-1] += extra
    return pl.pallas_call(
        functools.partial(piece_kernel, columns, experts),
        out_shape=[jax.ShapeDtypeStruct((tok_rows, width), tokens.dtype) for width in widths],
    )(tokens, expert_ids.T, gate_fixed.T)


def per_device(tokens, gate_weight, up_weight, down_weight, expert_ids, gate_fixed):
    experts = lax.axis_size("expert")
    bits = experts.bit_length() - 1
    tok_rows, top_count = expert_ids.shape
    feature_count = tokens.shape[1]
    gather, reduce, mirror = plan(experts)
    columns = split(feature_count, [share for _, share in gather])
    rows = experts * tok_rows

    own = [w[0] for w in (gate_weight, up_weight, down_weight)]
    far = [other_core(w) for w in own[:1]]

    held = [
        piece.reshape((1,) * bits + piece.shape)
        for piece in cut_pieces(tokens, expert_ids, gate_fixed, columns, experts)
    ]
    for step in range(bits):
        for i, (order, _) in enumerate(gather):
            axis = order[step]
            held[i] = jnp.concatenate([held[i], cross(held[i], axis, experts, mirror)], axis=axis)
    held = [piece.reshape(rows, -1) for piece in held]
    held[0], near = lax.optimization_barrier((held[0], own[1]))
    far.append(other_core(near))
    held[0], near = lax.optimization_barrier((held[0], own[2]))
    far.append(other_core(near))

    mine = lax.axis_index("expert")
    shares = held[-1][:, columns[-1][1] :]
    lane = jnp.arange(shares.shape[1], dtype=jnp.int32)
    picked = (lane == mine) | (lane == mine + experts)
    weight = jnp.sum(jnp.where(picked[None, :], shares.astype(jnp.float32), 0.0), axis=1, keepdims=True)

    def project(matrix):
        total = None
        for i in range(len(columns)):
            start, width = columns[i]
            part = jnp.dot(held[i][:, :width], matrix[start : start + width], preferred_element_type=jnp.float32)
            total = part if total is None else total + part
        return total

    hidden = [(jax.nn.silu(project(w[0])) * project(w[1])).astype(jnp.bfloat16) for w in (own, far)]

    sums = []
    for start, width in split(feature_count, [share for _, share in reduce]):
        part = sum(
            jnp.dot(h, w[2][:, start : start + width], preferred_element_type=jnp.float32)
            for h, w in zip(hidden, (own, far))
        )
        sums.append((part * weight).astype(jnp.bfloat16).reshape((2,) * bits + (tok_rows, width)))
    sums = lax.optimization_barrier(sums)
    for step in reversed(range(bits)):
        for i, (order, _) in enumerate(reduce):
            axis = order[step]
            keep = lax.slice_in_dim(sums[i], 0, 1, axis=axis)
            arrived = cross(lax.slice_in_dim(sums[i], 1, 2, axis=axis), axis, experts, mirror)
            sums[i] = (keep.astype(jnp.float32) + arrived.astype(jnp.float32)).astype(jnp.bfloat16)
    return jnp.concatenate([part.reshape(tok_rows, -1) for part in sums], axis=1)


def solution(mesh):
    in_specs = (
        P(("groups", "expert", "sub"), None),
        P("expert", None, "sub"),
        P("expert", None, "sub"),
        P("expert", "sub", None),
        P(("groups", "expert", "sub"), None),
        P(("groups", "expert", "sub"), None),
    )
    out_specs = P(("groups", "expert", "sub"), None)
    return jax.shard_map(
        per_device, mesh=mesh, in_specs=in_specs, out_specs=out_specs, check_vma=False
    )
```

```python
import functools

import jax
import jax.numpy as jnp
from jax import lax
from jax.experimental import pallas as pl
from jax.sharding import PartitionSpec as P

LANES = 128
DEPTH_TILE = 256


def split(feature_count, parts):
    tiles = feature_count // DEPTH_TILE
    edges = [DEPTH_TILE * (tiles * sum(parts[:i]) // sum(parts)) for i in range(len(parts))] + [feature_count]
    return [(low, high - low) for low, high in zip(edges, edges[1:])]


def plan(experts):
    bits = experts.bit_length() - 1
    if experts == 16:
        gather = (((3, 0, 1, 2), 5), ((3, 1, 2, 0), 5), ((3, 2, 0, 1), 4))
        reduce = (((3, 1, 2, 0), 5), ((3, 2, 0, 1), 5), ((3, 0, 1, 2), 4))
        mirror = (1, 0, 2, 3)
    else:
        turns = range(0, bits, max(1, bits // 4))
        gather = tuple((tuple((turn + step) % bits for step in range(bits)), 1) for turn in turns)[:4]
        reduce = gather
        half = bits // 2
        mirror = tuple((bit + half) % bits if bits % 2 == 0 else bit for bit in range(bits))
    return gather, reduce, mirror


def cross(block, bit, experts, mirror):
    pairs = []
    for chip in range(experts):
        for core, flipped in ((0, bit), (1, mirror[bit])):
            pairs.append((chip * 2 + core, (chip ^ (1 << flipped)) * 2 + core))
    return lax.ppermute(block, ("expert", "sub"), pairs)


def other_core(block):
    return lax.ppermute(block, "sub", [(0, 1), (1, 0)])


def piece_kernel(columns, experts, tokens_ref, ids_ref, fixed_ref, *out_refs):
    for out_ref, (start, width) in zip(out_refs, columns):
        out_ref[:, :width] = tokens_ref[:, start : start + width]
    last_ref, width = out_refs[-1], columns[-1][1]
    fixed_point = fixed_ref[...].T.astype(jnp.float32)
    ids = ids_ref[...].T
    share = fixed_point / jnp.sum(fixed_point, axis=1, keepdims=True)
    lane = lax.broadcasted_iota(jnp.int32, (tokens_ref.shape[0], last_ref.shape[1] - width), 1)
    expert = jnp.where(lane < experts, lane, lane - experts)
    dense = jnp.zeros(lane.shape, jnp.float32)
    for k in range(share.shape[1]):
        dense = dense + jnp.where(expert == ids[:, k : k + 1], share[:, k : k + 1], 0.0)
    high = dense.astype(jnp.bfloat16).astype(jnp.float32)
    last_ref[:, width:] = jnp.where(lane < experts, high, dense - high).astype(last_ref.dtype)


def cut_pieces(tokens, expert_ids, gate_fixed, columns, experts):
    tok_rows = tokens.shape[0]
    extra = -(-2 * experts // LANES) * LANES
    widths = [width for _, width in columns]
    widths[-1] += extra
    return pl.pallas_call(
        functools.partial(piece_kernel, columns, experts),
        out_shape=[jax.ShapeDtypeStruct((tok_rows, width), tokens.dtype) for width in widths],
    )(tokens, expert_ids.T, gate_fixed.T)


def per_device(tokens, gate_weight, up_weight, down_weight, expert_ids, gate_fixed):
    experts = lax.axis_size("expert")
    bits = experts.bit_length() - 1
    tok_rows, top_count = expert_ids.shape
    feature_count = tokens.shape[1]
    gather, reduce, mirror = plan(experts)
    columns = split(feature_count, [share for _, share in gather])
    rows = experts * tok_rows

    own = [w[0] for w in (gate_weight, up_weight, down_weight)]
    far = []

    held = [
        piece.reshape((1,) * bits + piece.shape)
        for piece in cut_pieces(tokens, expert_ids, gate_fixed, columns, experts)
    ]
    for step in range(bits):
        for i, (order, _) in enumerate(gather):
            axis = order[step]
            held[i] = jnp.concatenate([held[i], cross(held[i], axis, experts, mirror)], axis=axis)
        if step == bits - 2:
            held[0], near = lax.optimization_barrier((held[0], own[0]))
            far.append(other_core(near))
    held = [piece.reshape(rows, -1) for piece in held]
    held[0], near = lax.optimization_barrier((held[0], own[1]))
    far.append(other_core(near))
    held[0], near = lax.optimization_barrier((held[0], own[2]))
    far.append(other_core(near))

    mine = lax.axis_index("expert")
    shares = held[-1][:, columns[-1][1] :]
    lane = jnp.arange(shares.shape[1], dtype=jnp.int32)
    picked = (lane == mine) | (lane == mine + experts)
    weight = jnp.sum(jnp.where(picked[None, :], shares.astype(jnp.float32), 0.0), axis=1, keepdims=True)

    def project(matrix):
        total = None
        for i in range(len(columns)):
            start, width = columns[i]
            part = jnp.dot(held[i][:, :width], matrix[start : start + width], preferred_element_type=jnp.float32)
            total = part if total is None else total + part
        return total

    hidden = [(jax.nn.silu(project(w[0])) * project(w[1])).astype(jnp.bfloat16) for w in (own, far)]

    sums = []
    for start, width in split(feature_count, [share for _, share in reduce]):
        part = sum(
            jnp.dot(h, w[2][:, start : start + width], preferred_element_type=jnp.float32)
            for h, w in zip(hidden, (own, far))
        )
        sums.append((part * weight).astype(jnp.bfloat16).reshape((2,) * bits + (tok_rows, width)))
    sums = lax.optimization_barrier(sums)
    for step in reversed(range(bits)):
        for i, (order, _) in enumerate(reduce):
            axis = order[step]
            keep = lax.slice_in_dim(sums[i], 0, 1, axis=axis)
            arrived = cross(lax.slice_in_dim(sums[i], 1, 2, axis=axis), axis, experts, mirror)
            sums[i] = (keep.astype(jnp.float32) + arrived.astype(jnp.float32)).astype(jnp.bfloat16)
    return jnp.concatenate([part.reshape(tok_rows, -1) for part in sums], axis=1)


def solution(mesh):
    in_specs = (
        P(("groups", "expert", "sub"), None),
        P("expert", None, "sub"),
        P("expert", None, "sub"),
        P("expert", "sub", None),
        P(("groups", "expert", "sub"), None),
        P(("groups", "expert", "sub"), None),
    )
    out_specs = P(("groups", "expert", "sub"), None)
    return jax.shard_map(
        per_device, mesh=mesh, in_specs=in_specs, out_specs=out_specs, check_vma=False
    )
```

```python
import functools

import jax
import jax.numpy as jnp
from jax import lax
from jax.experimental import pallas as pl
from jax.sharding import PartitionSpec as P

LANES = 128
DEPTH_TILE = 256


def split(feature_count, parts):
    tiles = feature_count // DEPTH_TILE
    edges = [DEPTH_TILE * (tiles * sum(parts[:i]) // sum(parts)) for i in range(len(parts))] + [feature_count]
    return [(low, high - low) for low, high in zip(edges, edges[1:])]


def plan(experts):
    bits = experts.bit_length() - 1
    if experts == 16:
        gather = (((3, 0, 1, 2), 5), ((3, 1, 2, 0), 5), ((3, 2, 0, 1), 4))
        reduce = (((3, 1, 2, 0), 5), ((3, 2, 0, 1), 5), ((3, 0, 1, 2), 4))
        mirror = (1, 0, 2, 3)
    else:
        turns = range(0, bits, max(1, bits // 4))
        gather = tuple((tuple((turn + step) % bits for step in range(bits)), 1) for turn in turns)[:4]
        reduce = gather
        half = bits // 2
        mirror = tuple((bit + half) % bits if bits % 2 == 0 else bit for bit in range(bits))
    return gather, reduce, mirror


def cross(block, bit, experts, mirror):
    pairs = []
    for chip in range(experts):
        for core, flipped in ((0, bit), (1, mirror[bit])):
            pairs.append((chip * 2 + core, (chip ^ (1 << flipped)) * 2 + core))
    return lax.ppermute(block, ("expert", "sub"), pairs)


def other_core(block):
    return lax.ppermute(block, "sub", [(0, 1), (1, 0)])


def piece_kernel(columns, experts, tokens_ref, ids_ref, fixed_ref, *out_refs):
    for out_ref, (start, width) in zip(out_refs, columns):
        out_ref[:, :width] = tokens_ref[:, start : start + width]
    last_ref, width = out_refs[-1], columns[-1][1]
    fixed_point = fixed_ref[...].T.astype(jnp.float32)
    ids = ids_ref[...].T
    share = fixed_point / jnp.sum(fixed_point, axis=1, keepdims=True)
    lane = lax.broadcasted_iota(jnp.int32, (tokens_ref.shape[0], last_ref.shape[1] - width), 1)
    expert = jnp.where(lane < experts, lane, lane - experts)
    dense = jnp.zeros(lane.shape, jnp.float32)
    for k in range(share.shape[1]):
        dense = dense + jnp.where(expert == ids[:, k : k + 1], share[:, k : k + 1], 0.0)
    high = dense.astype(jnp.bfloat16).astype(jnp.float32)
    last_ref[:, width:] = jnp.where(lane < experts, high, dense - high).astype(last_ref.dtype)


def cut_pieces(tokens, expert_ids, gate_fixed, columns, experts):
    tok_rows = tokens.shape[0]
    extra = -(-2 * experts // LANES) * LANES
    widths = [width for _, width in columns]
    widths[-1] += extra
    return pl.pallas_call(
        functools.partial(piece_kernel, columns, experts),
        out_shape=[jax.ShapeDtypeStruct((tok_rows, width), tokens.dtype) for width in widths],
    )(tokens, expert_ids.T, gate_fixed.T)


def per_device(tokens, gate_weight, up_weight, down_weight, expert_ids, gate_fixed):
    experts = lax.axis_size("expert")
    bits = experts.bit_length() - 1
    tok_rows, top_count = expert_ids.shape
    feature_count = tokens.shape[1]
    gather, reduce, mirror = plan(experts)
    columns = split(feature_count, [share for _, share in gather])
    rows = experts * tok_rows

    own = [w[0] for w in (gate_weight, up_weight, down_weight)]
    far = []

    held = [
        piece.reshape((1,) * bits + piece.shape)
        for piece in cut_pieces(tokens, expert_ids, gate_fixed, columns, experts)
    ]
    for step in range(bits):
        for i, (order, _) in enumerate(gather):
            axis = order[step]
            held[i] = jnp.concatenate([held[i], cross(held[i], axis, experts, mirror)], axis=axis)
        if step == bits - 2:
            held[0], near = lax.optimization_barrier((held[0], own[0]))
            far.append(other_core(near))
            held[1], near = lax.optimization_barrier((held[1], own[1]))
            far.append(other_core(near))
    held = [piece.reshape(rows, -1) for piece in held]
    held[0], near = lax.optimization_barrier((held[0], own[2]))
    far.append(other_core(near))

    mine = lax.axis_index("expert")
    shares = held[-1][:, columns[-1][1] :]
    lane = jnp.arange(shares.shape[1], dtype=jnp.int32)
    picked = (lane == mine) | (lane == mine + experts)
    weight = jnp.sum(jnp.where(picked[None, :], shares.astype(jnp.float32), 0.0), axis=1, keepdims=True)

    def project(matrix):
        total = None
        for i in range(len(columns)):
            start, width = columns[i]
            part = jnp.dot(held[i][:, :width], matrix[start : start + width], preferred_element_type=jnp.float32)
            total = part if total is None else total + part
        return total

    hidden = [(jax.nn.silu(project(w[0])) * project(w[1])).astype(jnp.bfloat16) for w in (own, far)]

    sums = []
    for start, width in split(feature_count, [share for _, share in reduce]):
        part = sum(
            jnp.dot(h, w[2][:, start : start + width], preferred_element_type=jnp.float32)
            for h, w in zip(hidden, (own, far))
        )
        sums.append((part * weight).astype(jnp.bfloat16).reshape((2,) * bits + (tok_rows, width)))
    sums = lax.optimization_barrier(sums)
    for step in reversed(range(bits)):
        for i, (order, _) in enumerate(reduce):
            axis = order[step]
            keep = lax.slice_in_dim(sums[i], 0, 1, axis=axis)
            arrived = cross(lax.slice_in_dim(sums[i], 1, 2, axis=axis), axis, experts, mirror)
            sums[i] = (keep.astype(jnp.float32) + arrived.astype(jnp.float32)).astype(jnp.bfloat16)
    return jnp.concatenate([part.reshape(tok_rows, -1) for part in sums], axis=1)


def solution(mesh):
    in_specs = (
        P(("groups", "expert", "sub"), None),
        P("expert", None, "sub"),
        P("expert", None, "sub"),
        P("expert", "sub", None),
        P(("groups", "expert", "sub"), None),
        P(("groups", "expert", "sub"), None),
    )
    out_specs = P(("groups", "expert", "sub"), None)
    return jax.shard_map(
        per_device, mesh=mesh, in_specs=in_specs, out_specs=out_specs, check_vma=False
    )
```
